32 devices in a mesh: groups: 2 (over y), rows: 8 (over z, x), sub: 2 (over core).
Axes of the slice: x: 2, y: 2, z: 4, core: 2. Of those that a mesh axis runs over, the one named last changes fastest.
Arguments:
- coupling: bfloat16 [131072, 128], P(('groups', 'rows', 'sub')), parts along dimension 0, may hold values from 0.009 to 110
- tile_vals: bfloat16 [1024, 6, 128, 128], P(('groups', 'rows', 'sub')), parts along dimension 0, may hold values from -0.02734375 to 0.02734375
- tile_cols: int32 [1024, 6], P(('groups', 'rows', 'sub')), parts along dimension 0, may hold values from 0 to 511, as said below
- cluster_graph: int32 [256, 128], P('groups'), parts along dimension 0, may hold values from 0 to 3
- cluster_mass: float32 [256], P('groups'), parts along dimension 0, may hold values from 0.25 to 4
Outputs:
- log_coupling: float32 [131072, 128], P(('groups', 'rows', 'sub')), parts along dimension 0
The draws below stay inside these ranges and needn't reach their ends.
There are 2 independent parts, one for each index of `groups`. The reference program is written for one: setup_inputs(seed, part) draws one part's arguments, and reference() takes and returns one part's arrays. A program takes and returns all parts, laid end to end along the dimension named above; each array names one. Nothing has to cross between parts.
Inputs may be any that keep to these rules, and one draw needn't show every extreme that they name: `tile_cols`: within each device's rows of 32 block rows, a slot below 4 names a column block held by the same device or by the device just before or after it along rows+sub. Over the slots from 4 on, the block rows of one device name column blocks held by any one device at most 4 times, and some device exactly 4 times.
All inputs are finite; a program needn't handle non-finite values.
Results may differ from the reference program's by a relative error of at most 0.0003.
Values may be sent and summed in bfloat16 or wider, within the bound.
A program may use at most 128 MiB of HBM per device.

```python
import math
import jax
import jax.numpy as jnp
from jax import lax

K = 128
BLK = 128
SLOTS = 6
NEAR = 4
FAR = 2
NB = 32
SHARDS = 16
NBLK = 512
NODES = 65536


def draw_tile_cols(key, part):
    key_near = jax.random.fold_in(key, 11)
    key_owner = jax.random.fold_in(key, 12)
    key_order = jax.random.fold_in(key, 13)
    key_local = jax.random.fold_in(key, 14)
    block_ids = jnp.arange(NBLK, dtype=jnp.int32)
    home_block = block_ids // NB * NB
    near_cols = home_block[:, None] - NB + jax.random.randint(key_near, (NBLK, NEAR), 0, 3 * NB)
    near_cols = jnp.clip(near_cols, 0, NBLK - 1)
    far_count = NB * FAR
    owners = jax.random.permutation(key_owner, SHARDS).astype(jnp.int32)
    listed = owners[jnp.arange(far_count, dtype=jnp.int32) % SHARDS]
    order_keys = jax.random.split(key_order, SHARDS)
    orders = jax.vmap(lambda one_key: jax.random.permutation(one_key, far_count))(order_keys)
    far_owner = listed[orders]
    far_cols = far_owner * NB + jax.random.randint(key_local, (SHARDS, far_count), 0, NB)
    far_cols = far_cols.reshape(NBLK, FAR)
    return jnp.concatenate([near_cols, far_cols], axis=1).astype(jnp.int32)


def draw_coupling(key, part):
    key_rough = jax.random.fold_in(key, 21)
    key_slope = jax.random.fold_in(key, 22)
    rough = jnp.clip(0.8 * jax.random.normal(key_rough, (NODES, K), jnp.float32), -2.4, 2.4)
    slope = jax.random.uniform(key_slope, (K,), jnp.float32, -2.2, 2.2)
    place = jnp.arange(NODES, dtype=jnp.float32) / NODES - 0.5
    return jnp.exp(rough + 2.0 * place[:, None] * slope[None, :]).astype(jnp.bfloat16)


def with_ends(drawn, key, least, high):
    dims = drawn.shape
    spot = [jax.random.randint(jax.random.fold_in(key, axis), (), 0, dims[axis]) for axis in range(len(dims))]
    drawn = drawn.at[tuple(spot)].set(least)
    longest = dims.index(max(dims))
    spot[longest] = (spot[longest] + 1) % dims[longest]
    return drawn.at[tuple(spot)].set(high)


def shard_levels(own_key, shape, cuts, least, top_value):
    loudness, own = 1.0, jax.random.fold_in(own_key, 6)
    for dim, blocks in cuts:
        heights = jnp.exp(jax.random.uniform(jax.random.fold_in(own, dim), (blocks,), jnp.float32, least / len(cuts), top_value / len(cuts)))
        loudness = loudness * jnp.repeat(heights, shape[dim] // blocks).reshape([-1 if axis == dim else 1 for axis in range(len(shape))])
    return loudness


def gaussian(rng, extent, width, limit, shards=(), held_as=jnp.bfloat16):
    values = width * jax.random.normal(rng, extent, jnp.float32)
    if shards:
        values = values * shard_levels(rng, extent, shards, -0.22, 0.18)
    return jnp.clip(values, -limit, limit).astype(held_as)


def setup_inputs(seed: int = 0, part: int = 0) -> dict:
    splits = jax.random.split(jax.random.key(seed), 6)
    own_keys = jax.random.split(jax.random.fold_in(splits[5], part), 6)
    coupling = draw_coupling(jax.random.fold_in(jax.random.fold_in(splits[5], part), 71), part)
    tile_vals = gaussian(own_keys[1], (NBLK, SLOTS, BLK, BLK), (64 * BLK * SLOTS) ** -0.5, 0.02734375, ((0, 16),))
    tile_cols = draw_tile_cols(jax.random.fold_in(jax.random.fold_in(splits[5], part), 71), part)
    cluster_graph = with_ends(jax.random.randint(own_keys[3], (K, K), 0, 4), jax.random.fold_in(own_keys[3], 1), 0, 3).astype(jnp.int32)
    cluster_mass = jnp.clip(jnp.exp(jax.random.uniform(own_keys[4], (K,), jnp.float32, math.log(0.25), math.log(4.0))), 0.25, 4.0)
    return {"coupling": coupling, "tile_vals": tile_vals, "tile_cols": tile_cols, "cluster_graph": cluster_graph, "cluster_mass": cluster_mass}


eta_step = 2.0
relax_power = 0.5


def reference(coupling, tile_vals, tile_cols, cluster_graph, cluster_mass):
    blocks = coupling.reshape(NBLK, BLK, K).astype(jnp.float32)
    spread = jnp.zeros((NBLK, BLK, K), jnp.float32)
    for slot_id in range(SLOTS):
        picked = jnp.take(blocks, tile_cols[:, slot_id].astype(jnp.int32), axis=0)
        spread = spread + jnp.einsum("nij,njk->nik", tile_vals[:, slot_id].astype(jnp.float32), picked, precision=lax.Precision.HIGHEST)
    spread = spread.reshape(NODES, K)
    graph = cluster_graph.astype(jnp.float32)
    affinity = jnp.dot(spread, graph.T / K, precision=lax.Precision.HIGHEST)
    whole = coupling.astype(jnp.float32)
    colmass = jnp.sum(whole, axis=0) / NODES
    pull = jnp.dot(graph * graph, colmass, precision=lax.Precision.HIGHEST) / K
    logits = jnp.log(whole) - eta_step * (pull[None, :] - 2.0 * affinity)
    newmass = jnp.sum(jnp.exp(logits), axis=0) / NODES
    shifted = logits + relax_power * (jnp.log(cluster_mass) - jnp.log(newmass))[None, :]
    return shifted - jnp.log(jnp.sum(jnp.exp(shifted), axis=1, keepdims=True))
```

```python
import functools

import jax
import jax.numpy as jnp
from jax import lax
from jax.experimental import pallas as pl
from jax.experimental.pallas import tpu as pltpu
from jax.sharding import PartitionSpec as P

NEAR = 4

eta_step = 2.0
relax_power = 0.5
AXES = ("rows", "sub")


def kernel(
    shards,
    sub,
    far_slots,
    capacity,
    near_ref,
    place_ref,
    asker_ref,
    cpl,
    tiles_hbm,
    req,
    graph,
    cmass,
    out,
    window,
    tiles,
    packed,
    far,
    prod,
    asked,
    asked_s,
    mass_out,
    mass_in,
    new_out,
    new_in,
    graph_t,
    tile_sem,
    asked_sem,
    req_send,
    req_recv,
    near_send,
    near_recv,
    mass_send,
    mass_recv,
    far_send,
    far_recv,
    new_send,
    new_recv,
):
    blocks, size, clusters = cpl.shape
    slots = NEAR + far_slots
    nodes_total = blocks * size * shards
    group = lax.axis_index("groups")
    me = lax.axis_index("rows") * sub + lax.axis_index("sub")

    def where(peer):
        return (group, peer // sub, peer % sub)

    def remote(src, dst, send_sem, recv_sem, peer):
        return pltpu.make_async_remote_copy(
            src_ref=src,
            dst_ref=dst,
            send_sem=send_sem,
            recv_sem=recv_sem,
            device_id=where(peer),
            device_id_type=pl.DeviceIdType.MESH,
        )

    def offset(j):
        return shards // 2 + (1 - 2 * (j % 2)) * ((j + 1) // 2)

    def each_peer(body):
        def step(j, _):
            body((me + offset(j)) % shards)
            return 0

        lax.fori_loop(0, shards - 1, step, 0)

    def each_source(body):
        def step(j, _):
            body((me + shards - offset(j)) % shards)
            return 0

        lax.fori_loop(0, shards - 1, step, 0)

    tile_copy = pltpu.make_async_copy(tiles_hbm, tiles, tile_sem)
    tile_copy.start()

    barrier = pltpu.get_barrier_semaphore()
    each_peer(
        lambda peer: pl.semaphore_signal(
            barrier, inc=1, device_id=where(peer), device_id_type=pl.DeviceIdType.MESH
        )
    )
    asked[me] = req[me]
    pl.semaphore_wait(barrier, shards - 1)

    def req_copy(peer, slot):
        return remote(req.at[peer], asked.at[slot], req_send.at[peer], req_recv.at[slot], peer)

    each_peer(lambda peer: req_copy(peer, me).start())

    below = remote(cpl, window.at[pl.ds(2 * blocks, blocks)], near_send.at[0], near_recv.at[1], me - 1)
    above = remote(cpl, window.at[pl.ds(0, blocks)], near_send.at[1], near_recv.at[0], me + 1)

    @pl.when(me > 0)
    def _():
        below.start()

    @pl.when(me < shards - 1)
    def _():
        above.start()

    def mass_step(b, acc):
        block = cpl[b]
        window[blocks + b] = block
        return acc + jnp.sum(block.astype(jnp.float32).reshape(size // 8, 8, clusters), axis=0)

    acc = lax.fori_loop(0, blocks, mass_step, jnp.zeros((8, clusters), jnp.float32))
    mass_out[...] = jnp.sum(acc, axis=0, keepdims=True)
    mass_in[me] = mass_out[...]

    def mass_copy(peer, slot):
        return remote(mass_out, mass_in.at[slot], mass_send.at[peer], mass_recv.at[slot], peer)

    each_source(lambda peer: req_copy(peer, peer).wait_recv())
    asked_copy = pltpu.make_async_copy(asked, asked_s, asked_sem)
    asked_copy.start()
    asked_copy.wait()

    def far_copy(peer, slot):
        return remote(packed.at[peer], far.at[slot], far_send.at[peer], far_recv.at[slot], peer)

    def pack(peer):
        for s in range(capacity):
            packed[peer, s] = cpl[asked_s[peer, 0, s]]
        far_copy(peer, me).start()

    each_peer(pack)
    for s in range(capacity):
        far[me, s] = cpl[asked_s[me, 0, s]]
    each_peer(lambda peer: mass_copy(peer, me).start())

    graph_f = graph[...].astype(jnp.float32)
    turned = graph_f.T.astype(jnp.bfloat16)
    graph_t[pl.ds(0, clusters)] = turned
    graph_t[pl.ds(clusters, clusters)] = turned
    tile_copy.wait()

    @pl.when(me > 0)
    def _():
        above.wait_recv()

    @pl.when(me < shards - 1)
    def _():
        below.wait_recv()

    def near_step(b, _):
        left = jnp.concatenate([tiles[b * slots + s] for s in range(NEAR)], axis=1)
        right = jnp.concatenate([window[near_ref[b * NEAR + s]] for s in range(NEAR)], axis=0)
        out[b] = jnp.dot(left, right, preferred_element_type=jnp.float32)
        return 0

    lax.fori_loop(0, blocks, near_step, 0)

    def far_products(owner):
        for s in range(capacity):
            prod[owner * capacity + s] = jnp.dot(
                tiles[asker_ref[owner * capacity + s]],
                far[owner, s],
                preferred_element_type=jnp.float32,
            )

    far_products(me)
    each_source(lambda peer: mass_copy(peer, peer).wait_recv())
    colmass = jnp.sum(mass_in[...], axis=0) / nodes_total
    pull = (
        lax.dot_general(
            jnp.broadcast_to(colmass, (8, clusters)),
            graph_f * graph_f,
            (((1,), (1,)), ((), ())),
            precision=lax.Precision.HIGHEST,
            preferred_element_type=jnp.float32,
        )[:1]
        / clusters
    )

    def arrive(owner):
        far_copy(owner, owner).wait_recv()
        far_products(owner)

    each_source(arrive)

    def logit_step(b, acc):
        spread = out[b]
        for f in range(far_slots):
            spread = spread + prod[place_ref[b * far_slots + f]]
        high = spread.astype(jnp.bfloat16)
        low = (spread - high.astype(jnp.float32)).astype(jnp.bfloat16)
        affinity = jnp.dot(
            jnp.concatenate([high, low], axis=1), graph_t[...], preferred_element_type=jnp.float32
        ) / clusters
        logits = jnp.log(cpl[b].astype(jnp.float32)) - eta_step * (pull - 2.0 * affinity)
        out[b] = logits
        return acc + jnp.sum(jnp.exp(logits).reshape(size // 8, 8, clusters), axis=0)

    acc = lax.fori_loop(0, blocks, logit_step, jnp.zeros((8, clusters), jnp.float32))
    new_out[...] = jnp.sum(acc, axis=0, keepdims=True)
    new_in[me] = new_out[...]

    def new_copy(peer, slot):
        return remote(new_out, new_in.at[slot], new_send.at[peer], new_recv.at[slot], peer)

    each_peer(lambda peer: new_copy(peer, me).start())
    each_source(lambda peer: new_copy(peer, peer).wait_recv())
    newmass = jnp.sum(new_in[...], axis=0) / nodes_total
    shift = relax_power * (jnp.log(cmass[...]) - jnp.log(newmass))

    def final_step(b, _):
        shifted = out[b] + shift
        out[b] = shifted - jnp.log(jnp.sum(jnp.exp(shifted), axis=1, keepdims=True))
        return 0

    lax.fori_loop(0, blocks, final_step, 0)

    def drain(peer):
        req_copy(peer, peer).wait_send()
        mass_copy(peer, peer).wait_send()
        far_copy(peer, peer).wait_send()
        new_copy(peer, peer).wait_send()

    each_peer(drain)

    @pl.when(me > 0)
    def _():
        below.wait_send()

    @pl.when(me < shards - 1)
    def _():
        above.wait_send()


def local(coupling, tile_vals, tile_cols, cluster_graph, cluster_mass):
    shards = lax.axis_size(AXES)
    sub = lax.axis_size("sub")
    me = lax.axis_index(AXES)
    blocks, slots = tile_cols.shape
    size = tile_vals.shape[2]
    clusters = coupling.shape[1]
    far_slots = slots - NEAR
    far_count = blocks * far_slots
    capacity = (far_count + shards - 1) // shards
    near_index = (tile_cols[:, :NEAR] - (me * blocks - blocks)).reshape(blocks * NEAR)
    far_cols = tile_cols[:, NEAR:].reshape(far_count)
    owner = far_cols // blocks
    entry = jnp.arange(far_count, dtype=jnp.int32)
    earlier = (owner[:, None] == owner[None, :]) & (entry[:, None] > entry[None, :])
    place = owner * capacity + jnp.sum(earlier.astype(jnp.int32), axis=1)
    held = place[None, :] == jnp.arange(shards * capacity, dtype=jnp.int32)[:, None]
    asker = jnp.sum(
        jnp.where(held, (entry // far_slots * slots + NEAR + entry % far_slots)[None, :], 0), axis=1
    )
    asked = jnp.sum(jnp.where(held, (far_cols % blocks)[None, :], 0), axis=1)
    req = jnp.pad(asked.reshape(shards, 1, capacity), ((0, 0), (0, 0), (0, 128 - capacity)))

    vmem = pl.BlockSpec(memory_space=pltpu.VMEM)
    smem = pl.BlockSpec(memory_space=pltpu.SMEM)
    dma = pltpu.SemaphoreType.DMA
    out = pl.pallas_call(
        functools.partial(kernel, shards, sub, far_slots, capacity),
        out_shape=jax.ShapeDtypeStruct((blocks, size, clusters), jnp.float32),
        in_specs=[smem, smem, smem, vmem, pl.BlockSpec(memory_space=pl.ANY), vmem, vmem, vmem],
        out_specs=vmem,
        scratch_shapes=[
            pltpu.VMEM((3 * blocks, size, clusters), jnp.bfloat16),
            pltpu.VMEM((blocks * slots, size, size), jnp.bfloat16),
            pltpu.VMEM((shards, capacity, size, clusters), jnp.bfloat16),
            pltpu.VMEM((shards, capacity, size, clusters), jnp.bfloat16),
            pltpu.VMEM((shards * capacity, size, clusters), jnp.float32),
            pltpu.VMEM((shards, 1, 128), jnp.int32),
            pltpu.SMEM((shards, 1, 128), jnp.int32),
            pltpu.VMEM((1, clusters), jnp.float32),
            pltpu.VMEM((shards, 1, clusters), jnp.float32),
            pltpu.VMEM((1, clusters), jnp.float32),
            pltpu.VMEM((shards, 1, clusters), jnp.float32),
            pltpu.VMEM((2 * clusters, clusters), jnp.bfloat16),
            dma,
            dma,
            dma((shards,)),
            dma((shards,)),
            dma((2,)),
            dma((2,)),
            dma((shards,)),
            dma((shards,)),
            dma((shards,)),
            dma((shards,)),
            dma((shards,)),
            dma((shards,)),
        ],
        compiler_params=pltpu.CompilerParams(
            collective_id=0, has_side_effects=True, vmem_limit_bytes=48 * 2**20
        ),
        name="partition_step",
    )(
        near_index,
        place,
        asker,
        coupling.reshape(blocks, size, clusters),
        tile_vals.reshape(blocks * slots, size, size),
        req,
        cluster_graph,
        cluster_mass.reshape(1, clusters),
    )
    return out.reshape(blocks * size, clusters)


def solution(mesh):
    return jax.shard_map(
        local,
        mesh=mesh,
        in_specs=(
            P(("groups", "rows", "sub"), None),
            P(("groups", "rows", "sub"), None, None, None),
            P(("groups", "rows", "sub"), None),
            P("groups", None),
            P("groups"),
        ),
        out_specs=P(("groups", "rows", "sub"), None),
        check_vma=False,
    )
```

```python
import functools

import jax
import jax.numpy as jnp
from jax import lax
from jax.experimental import pallas as pl
from jax.experimental.pallas import tpu as pltpu
from jax.sharding import PartitionSpec as P

NEAR = 4

eta_step = 2.0
relax_power = 0.5
AXES = ("rows", "sub")


def kernel(
    shards,
    sub,
    capacity,
    cpl_hbm,
    tiles_hbm,
    cols_hbm,
    graph_hbm,
    cmass_hbm,
    out_hbm,
    shift_hbm,
    out,
    shift_out,
    own,
    window,
    tiles,
    packed,
    far,
    prod,
    cols,
    cols_s,
    graph,
    cmass,
    table,
    table_s,
    ask_out,
    asked,
    asked_s,
    mass_out,
    mass_in,
    new_out,
    new_in,
    graph_t,
    local_sem,
    ask_sem,
    mass_sem,
    new_sem,
    out_sem,
    near_send,
    near_recv,
    far_send,
    far_recv,
):
    blocks, size, clusters = own.shape
    slots = cols.shape[1]
    far_slots = slots - NEAR
    nodes_total = blocks * size * shards
    group = lax.axis_index("groups")
    me = lax.axis_index("rows") * sub + lax.axis_index("sub")

    def where(peer):
        return (group, peer // sub, peer % sub)

    def remote(src, dst, send_sem, recv_sem, peer):
        return pltpu.make_async_remote_copy(
            src_ref=src,
            dst_ref=dst,
            send_sem=send_sem,
            recv_sem=recv_sem,
            device_id=where(peer),
            device_id_type=pl.DeviceIdType.MESH,
        )

    def offset(j):
        return shards // 2 + (1 - 2 * (j % 2)) * ((j + 1) // 2)

    def each_peer(body):
        def step(j, _):
            body((me + offset(j)) % shards)
            return 0

        lax.fori_loop(0, shards - 1, step, 0)

    def each_source(body):
        def step(j, _):
            body((me + shards - offset(j)) % shards)
            return 0

        lax.fori_loop(0, shards - 1, step, 0)

    other = (me + 1) % shards

    def spread_out(src, dst, sem):
        each_peer(lambda peer: remote(src, dst.at[me], sem.at[0], sem.at[1], peer).start())

    def all_rows(dst, sem):
        rows = dst.at[pl.ds(0, shards - 1)]
        return remote(rows, rows, sem.at[0], sem.at[1], other)

    cols_copy = pltpu.make_async_copy(cols_hbm, cols, local_sem.at[0])
    cols_s_copy = pltpu.make_async_copy(cols_hbm, cols_s, local_sem.at[1])
    own_copy = pltpu.make_async_copy(cpl_hbm, own, local_sem.at[2])
    middle_copy = pltpu.make_async_copy(cpl_hbm, window.at[pl.ds(blocks, blocks)], local_sem.at[3])
    graph_copy = pltpu.make_async_copy(graph_hbm, graph, local_sem.at[4])
    cmass_copy = pltpu.make_async_copy(cmass_hbm, cmass, local_sem.at[5])
    tile_copy = pltpu.make_async_copy(tiles_hbm, tiles, local_sem.at[6])
    for copy in (cols_copy, own_copy, cols_s_copy, graph_copy, cmass_copy, middle_copy, tile_copy):
        copy.start()

    barrier = pltpu.get_barrier_semaphore()
    each_peer(
        lambda peer: pl.semaphore_signal(
            barrier, inc=1, device_id=where(peer), device_id_type=pl.DeviceIdType.MESH
        )
    )

    cols_copy.wait()
    names = cols[...]
    sub_i = lax.broadcasted_iota(jnp.int32, (blocks, blocks), 0)
    lane_i = lax.broadcasted_iota(jnp.int32, (blocks, blocks), 1)
    column = [names[:, NEAR + f : NEAR + f + 1] for f in range(far_slots)]
    row = [
        jnp.sum(jnp.where(sub_i == lane_i, c, 0), axis=0, keepdims=True) for c in column
    ]
    owner_c = [lax.div(c, jnp.int32(blocks)) for c in column]
    owner_r = [lax.div(r, jnp.int32(blocks)) for r in row]
    width = ask_out.shape[1]
    spot = lax.broadcasted_iota(jnp.int32, (blocks, width), 1)
    entry = lax.broadcasted_iota(jnp.int32, (blocks, width), 0)
    asked_row = jnp.zeros((1, width), jnp.int32)
    asker_row = jnp.zeros((1, width), jnp.int32)
    for f in range(far_slots):
        rank_r = jnp.zeros((1, blocks), jnp.int32)
        rank_c = jnp.zeros((blocks, 1), jnp.int32)
        for g in range(far_slots):
            before = sub_i <= lane_i if g < f else sub_i < lane_i
            hit = (owner_c[g] == owner_r[f]) & before
            rank_r = rank_r + jnp.sum(hit.astype(jnp.int32), axis=0, keepdims=True)
            before = lane_i <= sub_i if g < f else lane_i < sub_i
            hit = (owner_c[f] == owner_r[g]) & before
            rank_c = rank_c + jnp.sum(hit.astype(jnp.int32), axis=1, keepdims=True)
        table[pl.ds(1 + f, 1), pl.ds(0, blocks)] = owner_r[f] * capacity + rank_r
        held = (owner_c[f] * capacity + rank_c) == spot
        asked_row = asked_row + jnp.sum(
            jnp.where(held, column[f] - owner_c[f] * blocks, 0), axis=0, keepdims=True
        )
        asker_row = asker_row + jnp.sum(
            jnp.where(held, entry * slots + (NEAR + f), 0), axis=0, keepdims=True
        )
    ask_out[...] = asked_row
    asked[me] = asked_row
    table[pl.ds(0, 1)] = asker_row
    table_copy = pltpu.make_async_copy(table, table_s, local_sem.at[7])
    table_copy.start()

    pl.semaphore_wait(barrier, shards - 1)
    spread_out(ask_out, asked, ask_sem)

    own_copy.wait()
    below = remote(own, window.at[pl.ds(2 * blocks, blocks)], near_send.at[0], near_recv.at[1], me - 1)
    above = remote(own, window.at[pl.ds(0, blocks)], near_send.at[1], near_recv.at[0], me + 1)

    @pl.when(me > 0)
    def _():
        below.start()

    @pl.when(me < shards - 1)
    def _():
        above.start()

    all_rows(asked, ask_sem).wait_recv()
    asked_copy = pltpu.make_async_copy(asked, asked_s, local_sem.at[8])
    asked_copy.start()
    asked_copy.wait()

    def far_copy(peer, slot):
        return remote(packed.at[peer], far.at[slot], far_send.at[peer], far_recv.at[slot], peer)

    def pack(peer):
        for s in range(capacity):
            packed[peer, s] = own[asked_s[peer, 0, me * capacity + s]]
        far_copy(peer, me).start()

    each_peer(pack)
    for s in range(capacity):
        far[me, s] = own[asked_s[me, 0, me * capacity + s]]

    def mass_step(b, acc):
        return acc + jnp.sum(own[b].astype(jnp.float32).reshape(size // 8, 8, clusters), axis=0)

    acc = lax.fori_loop(0, blocks, mass_step, jnp.zeros((8, clusters), jnp.float32))
    mass_out[...] = jnp.sum(acc, axis=0, keepdims=True)
    mass_in[me] = mass_out[...]
    spread_out(mass_out, mass_in, mass_sem)

    graph_copy.wait()
    graph_f = graph[...].astype(jnp.float32)
    turned = graph_f.T.astype(jnp.bfloat16)
    graph_t[pl.ds(0, clusters)] = turned
    graph_t[pl.ds(clusters, clusters)] = turned
    for copy in (tile_copy, cols_s_copy, table_copy, cmass_copy, middle_copy):
        copy.wait()

    def gain(spread):
        high = spread.astype(jnp.bfloat16)
        low = (spread - high.astype(jnp.float32)).astype(jnp.bfloat16)
        return jnp.dot(
            jnp.concatenate([high, low], axis=1), graph_t[...], preferred_element_type=jnp.float32
        ) * (2.0 * eta_step / clusters)

    all_rows(mass_in, mass_sem).wait_recv()
    colmass = jnp.sum(mass_in[...], axis=0) / nodes_total
    pull = (
        lax.dot_general(
            jnp.broadcast_to(colmass, (8, clusters)),
            graph_f * graph_f,
            (((1,), (1,)), ((), ())),
            precision=lax.Precision.HIGHEST,
            preferred_element_type=jnp.float32,
        )[:1]
        / clusters
    )

    @pl.when(me > 0)
    def _():
        above.wait_recv()

    @pl.when(me < shards - 1)
    def _():
        below.wait_recv()

    first = (me - 1) * blocks

    pair = 2 if blocks % 2 == 0 else 1

    def near_step(i, _):
        spread = []
        for u in range(pair):
            b = i * pair + u
            left = jnp.concatenate([tiles[b * slots + s] for s in range(NEAR)], axis=1)
            picked = [jnp.clip(cols_s[b, s] - first, 0, 3 * blocks - 1) for s in range(NEAR)]
            right = jnp.concatenate([window[p] for p in picked], axis=0)
            spread.append(jnp.dot(left, right, preferred_element_type=jnp.float32))
        added = gain(jnp.concatenate(spread, axis=0))
        for u in range(pair):
            b = i * pair + u
            base = jnp.log(own[b].astype(jnp.float32)) - eta_step * pull
            out[b] = base + added[u * size : (u + 1) * size]
        return 0

    lax.fori_loop(0, blocks // pair, near_step, 0)
    all_rows(asked, ask_sem).wait_send()
    all_rows(mass_in, mass_sem).wait_send()

    def far_products(owner):
        for s in range(capacity):
            place = owner * capacity + s
            prod[place] = jnp.dot(
                tiles[table_s[0, place]], far[owner, s], preferred_element_type=jnp.float32
            )

    far_products(me)

    def arrive(owner):
        far_copy(owner, owner).wait_recv()
        far_products(owner)

    each_source(arrive)

    parts = out_sem.shape[0] - 1
    each = blocks // parts
    group_of = next(u for u in (4, 2, 1) if each % u == 0)

    def out_copy(p):
        rows = pl.ds(p * each, each)
        return pltpu.make_async_copy(out.at[rows], out_hbm.at[rows], out_sem.at[p])

    def logit_step(p, i, acc):
        start = p * each + i * group_of
        spread = []
        for u in range(group_of):
            spread.append(prod[table_s[1, start + u]])
            for f in range(1, far_slots):
                spread[u] = spread[u] + prod[table_s[1 + f, start + u]]
        added = gain(jnp.concatenate(spread, axis=0))
        for u in range(group_of):
            logits = out[start + u] + added[u * size : (u + 1) * size]
            out[start + u] = logits
            acc = acc + jnp.sum(jnp.exp(logits).reshape(size // 8, 8, clusters), axis=0)
        return acc

    acc = jnp.zeros((8, clusters), jnp.float32)
    for p in range(parts):
        acc = lax.fori_loop(0, each // group_of, functools.partial(logit_step, p), acc)
        out_copy(p).start()
    new_out[...] = jnp.sum(acc, axis=0, keepdims=True)
    new_in[me] = new_out[...]
    spread_out(new_out, new_in, new_sem)

    each_peer(lambda peer: far_copy(peer, peer).wait_send())

    @pl.when(me > 0)
    def _():
        below.wait_send()

    @pl.when(me < shards - 1)
    def _():
        above.wait_send()

    for p in range(parts):
        out_copy(p).wait()
    all_rows(new_in, new_sem).wait_recv()
    newmass = jnp.sum(new_in[...], axis=0) / nodes_total
    shift_out[...] = relax_power * (jnp.log(cmass[...]) - jnp.log(newmass))
    shift_copy = pltpu.make_async_copy(shift_out, shift_hbm, out_sem.at[parts])
    shift_copy.start()
    shift_copy.wait()
    all_rows(new_in, new_sem).wait_send()


def finish(logits_hbm, shift_hbm, out_hbm, held, shift, in_sem, out_sem):
    blocks = held.shape[0]
    parts = out_sem.shape[0]
    each = blocks // parts
    group_of = next(u for u in (4, 2, 1) if each % u == 0)

    def fetch(p):
        rows = pl.ds(p * each, each)
        return pltpu.make_async_copy(logits_hbm.at[rows], held.at[rows], in_sem.at[p])

    def store(p):
        rows = pl.ds(p * each, each)
        return pltpu.make_async_copy(held.at[rows], out_hbm.at[rows], out_sem.at[p])

    shift_copy = pltpu.make_async_copy(shift_hbm, shift, in_sem.at[parts])
    shift_copy.start()
    for p in range(parts):
        fetch(p).start()
    shift_copy.wait()
    for p in range(parts):
        fetch(p).wait()

        def step(i, _):
            for u in range(group_of):
                b = p * each + i * group_of + u
                shifted = held[b] + shift[...]
                held[b] = shifted - jnp.log(jnp.sum(jnp.exp(shifted), axis=1, keepdims=True))
            return 0

        lax.fori_loop(0, each // group_of, step, 0)
        store(p).start()
    for p in range(parts):
        store(p).wait()


def local(coupling, tile_vals, tile_cols, cluster_graph, cluster_mass):
    shards = lax.axis_size(AXES)
    sub = lax.axis_size("sub")
    blocks, slots = tile_cols.shape
    size = tile_vals.shape[2]
    clusters = coupling.shape[1]
    far_slots = slots - NEAR
    capacity = (blocks * far_slots + shards - 1) // shards
    width = (shards * capacity + 127) // 128 * 128

    parts = next(u for u in (4, 2, 1) if blocks % u == 0)

    hbm = pl.BlockSpec(memory_space=pl.ANY)
    dma = pltpu.SemaphoreType.DMA
    logits, shift = pl.pallas_call(
        functools.partial(kernel, shards, sub, capacity),
        out_shape=(
            jax.ShapeDtypeStruct((blocks, size, clusters), jnp.float32),
            jax.ShapeDtypeStruct((1, clusters), jnp.float32),
        ),
        in_specs=[hbm] * 5,
        out_specs=(hbm, hbm),
        scratch_shapes=[
            pltpu.VMEM((blocks, size, clusters), jnp.float32),
            pltpu.VMEM((1, clusters), jnp.float32),
            pltpu.VMEM((blocks, size, clusters), jnp.bfloat16),
            pltpu.VMEM((3 * blocks, size, clusters), jnp.bfloat16),
            pltpu.VMEM((blocks * slots, size, size), jnp.bfloat16),
            pltpu.VMEM((shards, capacity, size, clusters), jnp.bfloat16),
            pltpu.VMEM((shards, capacity, size, clusters), jnp.bfloat16),
            pltpu.VMEM((shards * capacity, size, clusters), jnp.float32),
            pltpu.VMEM((blocks, slots), jnp.int32),
            pltpu.SMEM((blocks, slots), jnp.int32),
            pltpu.VMEM((clusters, clusters), jnp.int32),
            pltpu.VMEM((1, clusters), jnp.float32),
            pltpu.VMEM((8, width), jnp.int32),
            pltpu.SMEM((8, width), jnp.int32),
            pltpu.VMEM((1, width), jnp.int32),
            pltpu.VMEM((shards, 1, width), jnp.int32),
            pltpu.SMEM((shards, 1, width), jnp.int32),
            pltpu.VMEM((1, clusters), jnp.float32),
            pltpu.VMEM((shards, 1, clusters), jnp.float32),
            pltpu.VMEM((1, clusters), jnp.float32),
            pltpu.VMEM((shards, 1, clusters), jnp.float32),
            pltpu.VMEM((2 * clusters, clusters), jnp.bfloat16),
            dma((9,)),
            dma((2,)),
            dma((2,)),
            dma((2,)),
            dma((parts + 1,)),
            dma((2,)),
            dma((2,)),
            dma((shards,)),
            dma((shards,)),
        ],
        compiler_params=pltpu.CompilerParams(
            collective_id=0, has_side_effects=True, vmem_limit_bytes=56 * 2**20
        ),
        name="partition_step",
    )(
        coupling.reshape(blocks, size, clusters),
        tile_vals.reshape(blocks * slots, size, size),
        tile_cols,
        cluster_graph,
        cluster_mass.reshape(1, clusters),
    )
    out = pl.pallas_call(
        finish,
        out_shape=jax.ShapeDtypeStruct((blocks, size, clusters), jnp.float32),
        in_specs=[hbm, hbm],
        out_specs=hbm,
        scratch_shapes=[
            pltpu.VMEM((blocks, size, clusters), jnp.float32),
            pltpu.VMEM((1, clusters), jnp.float32),
            dma((parts + 1,)),
            dma((parts,)),
        ],
        compiler_params=pltpu.CompilerParams(vmem_limit_bytes=56 * 2**20),
        name="normalise",
    )(logits, shift)
    return out.reshape(blocks * size, clusters)


def solution(mesh):
    return jax.shard_map(
        local,
        mesh=mesh,
        in_specs=(
            P(("groups", "rows", "sub"), None),
            P(("groups", "rows", "sub"), None, None, None),
            P(("groups", "rows", "sub"), None),
            P("groups", None),
            P("groups"),
        ),
        out_specs=P(("groups", "rows", "sub"), None),
        check_vma=False,
    )
```

```python
import functools

import jax
import jax.numpy as jnp
from jax import lax
from jax.experimental import pallas as pl
from jax.experimental.pallas import tpu as pltpu
from jax.sharding import PartitionSpec as P

NEAR = 4

eta_step = 2.0
relax_power = 0.5
AXES = ("rows", "sub")


def kernel(
    shards,
    sub,
    capacity,
    cpl_hbm,
    tiles_hbm,
    cols_hbm,
    graph_hbm,
    cmass_hbm,
    out_hbm,
    shift_hbm,
    out,
    shift_out,
    own,
    window,
    tiles,
    packed,
    far,
    prod,
    cols,
    cols_s,
    graph,
    cmass,
    table,
    table_s,
    ask_out,
    asked,
    asked_s,
    mass_out,
    mass_in,
    new_out,
    new_in,
    graph_t,
    local_sem,
    ask_sem,
    mass_sem,
    new_sem,
    out_sem,
    near_send,
    near_recv,
    far_send,
    far_recv,
):
    blocks, size, clusters = own.shape
    slots = cols.shape[0]
    far_slots = slots - NEAR
    nodes_total = blocks * size * shards
    group = lax.axis_index("groups")
    me = lax.axis_index("rows") * sub + lax.axis_index("sub")

    def where(peer):
        return (group, peer // sub, peer % sub)

    def remote(src, dst, send_sem, recv_sem, peer):
        return pltpu.make_async_remote_copy(
            src_ref=src,
            dst_ref=dst,
            send_sem=send_sem,
            recv_sem=recv_sem,
            device_id=where(peer),
            device_id_type=pl.DeviceIdType.MESH,
        )

    half = shards // 2
    mine = me // half * half
    theirs = half - mine

    def each_peer(body):
        def step(j, _):
            other_half = 1 - j % 2
            body(mine + other_half * (theirs - mine) + (me + (j + 1) // 2) % half)
            return 0

        lax.fori_loop(0, shards - 1, step, 0)

    def each_source(body):
        def step(j, _):
            other_half = 1 - j % 2
            body(mine + other_half * (theirs - mine) + (me + half - (j + 1) // 2) % half)
            return 0

        lax.fori_loop(0, shards - 1, step, 0)

    other = (me + 1) % shards

    def spread_out(src, dst, sem):
        each_peer(lambda peer: remote(src, dst.at[me], sem.at[0], sem.at[1], peer).start())

    def all_rows(dst, sem):
        rows = dst.at[pl.ds(0, shards - 1)]
        return remote(rows, rows, sem.at[0], sem.at[1], other)

    cols_copy = pltpu.make_async_copy(cols_hbm, cols, local_sem.at[0])
    cols_s_copy = pltpu.make_async_copy(cols_hbm, cols_s, local_sem.at[1])
    own_copy = pltpu.make_async_copy(cpl_hbm, own, local_sem.at[2])
    middle_copy = pltpu.make_async_copy(cpl_hbm, window.at[pl.ds(blocks, blocks)], local_sem.at[3])
    graph_copy = pltpu.make_async_copy(graph_hbm, graph, local_sem.at[4])
    cmass_copy = pltpu.make_async_copy(cmass_hbm, cmass, local_sem.at[5])
    tile_copy = pltpu.make_async_copy(tiles_hbm, tiles, local_sem.at[6])
    for copy in (cols_copy, own_copy, cols_s_copy, graph_copy, cmass_copy, middle_copy, tile_copy):
        copy.start()

    barrier = pltpu.get_barrier_semaphore()
    each_peer(
        lambda peer: pl.semaphore_signal(
            barrier, inc=1, device_id=where(peer), device_id_type=pl.DeviceIdType.MESH
        )
    )

    cols_copy.wait()
    names = cols[...]
    sub_i = lax.broadcasted_iota(jnp.int32, (blocks, blocks), 0)
    lane_i = lax.broadcasted_iota(jnp.int32, (blocks, blocks), 1)
    row = [names[NEAR + f : NEAR + f + 1] for f in range(far_slots)]
    column = [
        jnp.sum(jnp.where(sub_i == lane_i, r, 0), axis=1, keepdims=True) for r in row
    ]
    owner_c = [lax.div(c, jnp.int32(blocks)) for c in column]
    owner_r = [lax.div(r, jnp.int32(blocks)) for r in row]
    width = ask_out.shape[1]
    spot = lax.broadcasted_iota(jnp.int32, (blocks, width), 1)
    entry = lax.broadcasted_iota(jnp.int32, (blocks, width), 0)
    asked_row = jnp.zeros((1, width), jnp.int32)
    asker_row = jnp.zeros((1, width), jnp.int32)
    for f in range(far_slots):
        rank_r = jnp.zeros((1, blocks), jnp.int32)
        rank_c = jnp.zeros((blocks, 1), jnp.int32)
        for g in range(far_slots):
            before = sub_i <= lane_i if g < f else sub_i < lane_i
            hit = (owner_c[g] == owner_r[f]) & before
            rank_r = rank_r + jnp.sum(hit.astype(jnp.int32), axis=0, keepdims=True)
            before = lane_i <= sub_i if g < f else lane_i < sub_i
            hit = (owner_c[f] == owner_r[g]) & before
            rank_c = rank_c + jnp.sum(hit.astype(jnp.int32), axis=1, keepdims=True)
        table[pl.ds(1 + f, 1), pl.ds(0, blocks)] = owner_r[f] * capacity + rank_r
        held = (owner_c[f] * capacity + rank_c) == spot
        asked_row = asked_row + jnp.sum(
            jnp.where(held, column[f] - owner_c[f] * blocks, 0), axis=0, keepdims=True
        )
        asker_row = asker_row + jnp.sum(
            jnp.where(held, entry * slots + (NEAR + f), 0), axis=0, keepdims=True
        )
    ask_out[...] = asked_row
    asked[me] = asked_row
    table[pl.ds(0, 1)] = asker_row
    table_copy = pltpu.make_async_copy(table, table_s, local_sem.at[7])
    table_copy.start()

    own_copy.wait()

    def mass_step(b, acc):
        return acc + jnp.sum(own[b].astype(jnp.float32).reshape(size // 8, 8, clusters), axis=0)

    acc = lax.fori_loop(0, blocks, mass_step, jnp.zeros((8, clusters), jnp.float32))
    mass_out[...] = jnp.sum(acc, axis=0, keepdims=True)
    mass_in[me] = mass_out[...]

    pl.semaphore_wait(barrier, shards - 1)
    spread_out(ask_out, asked, ask_sem)
    spread_out(mass_out, mass_in, mass_sem)
    below = remote(own, window.at[pl.ds(2 * blocks, blocks)], near_send.at[0], near_recv.at[1], me - 1)
    above = remote(own, window.at[pl.ds(0, blocks)], near_send.at[1], near_recv.at[0], me + 1)

    @pl.when(me > 0)
    def _():
        below.start()

    @pl.when(me < shards - 1)
    def _():
        above.start()

    all_rows(asked, ask_sem).wait_recv()
    asked_copy = pltpu.make_async_copy(asked, asked_s, local_sem.at[8])
    asked_copy.start()
    asked_copy.wait()

    def far_copy(peer, slot):
        return remote(packed.at[peer], far.at[slot], far_send.at[peer], far_recv.at[slot], peer)

    def pack(peer):
        for s in range(capacity):
            packed[peer, s] = own[asked_s[peer, 0, me * capacity + s]]
        far_copy(peer, me).start()

    each_peer(pack)
    for s in range(capacity):
        far[me, s] = own[asked_s[me, 0, me * capacity + s]]

    graph_copy.wait()
    graph_f = graph[...].astype(jnp.float32)
    turned = graph_f.T.astype(jnp.bfloat16)
    graph_t[pl.ds(0, clusters)] = turned
    graph_t[pl.ds(clusters, clusters)] = turned
    for copy in (tile_copy, cols_s_copy, table_copy, cmass_copy, middle_copy):
        copy.wait()

    def gain(spread):
        high = spread.astype(jnp.bfloat16)
        low = (spread - high.astype(jnp.float32)).astype(jnp.bfloat16)
        return jnp.dot(
            jnp.concatenate([high, low], axis=1), graph_t[...], preferred_element_type=jnp.float32
        ) * (2.0 * eta_step / clusters)

    all_rows(mass_in, mass_sem).wait_recv()
    colmass = jnp.sum(mass_in[...], axis=0) / nodes_total
    pull = (
        lax.dot_general(
            jnp.broadcast_to(colmass, (8, clusters)),
            graph_f * graph_f,
            (((1,), (1,)), ((), ())),
            precision=lax.Precision.HIGHEST,
            preferred_element_type=jnp.float32,
        )[:1]
        / clusters
    )

    @pl.when(me > 0)
    def _():
        above.wait_recv()

    @pl.when(me < shards - 1)
    def _():
        below.wait_recv()

    first = (me - 1) * blocks

    pair = 2 if blocks % 2 == 0 else 1

    def near_step(i, _):
        spread = []
        for u in range(pair):
            b = i * pair + u
            left = jnp.concatenate([tiles[b * slots + s] for s in range(NEAR)], axis=1)
            picked = [jnp.clip(cols_s[s, b] - first, 0, 3 * blocks - 1) for s in range(NEAR)]
            right = jnp.concatenate([window[p] for p in picked], axis=0)
            spread.append(jnp.dot(left, right, preferred_element_type=jnp.float32))
        added = gain(jnp.concatenate(spread, axis=0))
        for u in range(pair):
            b = i * pair + u
            base = jnp.log(own[b].astype(jnp.float32)) - eta_step * pull
            out[b] = base + added[u * size : (u + 1) * size]
        return 0

    lax.fori_loop(0, blocks // pair, near_step, 0)
    all_rows(asked, ask_sem).wait_send()
    all_rows(mass_in, mass_sem).wait_send()

    def far_products(owner):
        for s in range(capacity):
            place = owner * capacity + s
            prod[place] = jnp.dot(
                tiles[table_s[0, place]], far[owner, s], preferred_element_type=jnp.float32
            )

    far_products(me)

    def arrive(owner):
        far_copy(owner, owner).wait_recv()
        far_products(owner)

    each_source(arrive)

    parts = out_sem.shape[0] - 1
    each = blocks // parts
    group_of = next(u for u in (4, 2, 1) if each % u == 0)

    def out_copy(p):
        rows = pl.ds(p * each, each)
        return pltpu.make_async_copy(out.at[rows], out_hbm.at[rows], out_sem.at[p])

    def logit_step(p, i, acc):
        start = p * each + i * group_of
        spread = []
        for u in range(group_of):
            spread.append(prod[table_s[1, start + u]])
            for f in range(1, far_slots):
                spread[u] = spread[u] + prod[table_s[1 + f, start + u]]
        added = gain(jnp.concatenate(spread, axis=0))
        for u in range(group_of):
            logits = out[start + u] + added[u * size : (u + 1) * size]
            out[start + u] = logits
            acc = acc + jnp.sum(jnp.exp(logits).reshape(size // 8, 8, clusters), axis=0)
        return acc

    acc = jnp.zeros((8, clusters), jnp.float32)
    for p in range(parts):
        acc = lax.fori_loop(0, each // group_of, functools.partial(logit_step, p), acc)
        out_copy(p).start()
    new_out[...] = jnp.sum(acc, axis=0, keepdims=True)
    new_in[me] = new_out[...]
    spread_out(new_out, new_in, new_sem)

    each_peer(lambda peer: far_copy(peer, peer).wait_send())

    @pl.when(me > 0)
    def _():
        below.wait_send()

    @pl.when(me < shards - 1)
    def _():
        above.wait_send()

    for p in range(parts):
        out_copy(p).wait()
    all_rows(new_in, new_sem).wait_recv()
    newmass = jnp.sum(new_in[...], axis=0) / nodes_total
    shift_out[...] = relax_power * (jnp.log(cmass[...]) - jnp.log(newmass))
    shift_copy = pltpu.make_async_copy(shift_out, shift_hbm, out_sem.at[parts])
    shift_copy.start()
    shift_copy.wait()
    all_rows(new_in, new_sem).wait_send()


def finish(logits_hbm, shift_hbm, out_hbm, held, shift, in_sem, out_sem):
    blocks = held.shape[0]
    parts = out_sem.shape[0]
    each = blocks // parts
    group_of = next(u for u in (4, 2, 1) if each % u == 0)

    def fetch(p):
        rows = pl.ds(p * each, each)
        return pltpu.make_async_copy(logits_hbm.at[rows], held.at[rows], in_sem.at[p])

    def store(p):
        rows = pl.ds(p * each, each)
        return pltpu.make_async_copy(held.at[rows], out_hbm.at[rows], out_sem.at[p])

    shift_copy = pltpu.make_async_copy(shift_hbm, shift, in_sem.at[parts])
    shift_copy.start()
    for p in range(parts):
        fetch(p).start()
    shift_copy.wait()
    for p in range(parts):
        fetch(p).wait()

        def step(i, _):
            for u in range(group_of):
                b = p * each + i * group_of + u
                shifted = held[b] + shift[...]
                held[b] = shifted - jnp.log(jnp.sum(jnp.exp(shifted), axis=1, keepdims=True))
            return 0

        lax.fori_loop(0, each // group_of, step, 0)
        store(p).start()
    for p in range(parts):
        store(p).wait()


def local(coupling, tile_vals, tile_cols, cluster_graph, cluster_mass):
    shards = lax.axis_size(AXES)
    sub = lax.axis_size("sub")
    blocks, slots = tile_cols.shape
    size = tile_vals.shape[2]
    clusters = coupling.shape[1]
    far_slots = slots - NEAR
    capacity = (blocks * far_slots + shards - 1) // shards
    width = (shards * capacity + 127) // 128 * 128

    parts = next(u for u in (4, 2, 1) if blocks % u == 0)

    hbm = pl.BlockSpec(memory_space=pl.ANY)
    dma = pltpu.SemaphoreType.DMA
    logits, shift = pl.pallas_call(
        functools.partial(kernel, shards, sub, capacity),
        out_shape=(
            jax.ShapeDtypeStruct((blocks, size, clusters), jnp.float32),
            jax.ShapeDtypeStruct((1, clusters), jnp.float32),
        ),
        in_specs=[hbm] * 5,
        out_specs=(hbm, hbm),
        scratch_shapes=[
            pltpu.VMEM((blocks, size, clusters), jnp.float32),
            pltpu.VMEM((1, clusters), jnp.float32),
            pltpu.VMEM((blocks, size, clusters), jnp.bfloat16),
            pltpu.VMEM((3 * blocks, size, clusters), jnp.bfloat16),
            pltpu.VMEM((blocks * slots, size, size), jnp.bfloat16),
            pltpu.VMEM((shards, capacity, size, clusters), jnp.bfloat16),
            pltpu.VMEM((shards, capacity, size, clusters), jnp.bfloat16),
            pltpu.VMEM((shards * capacity, size, clusters), jnp.float32),
            pltpu.VMEM((slots, blocks), jnp.int32),
            pltpu.SMEM((slots, blocks), jnp.int32),
            pltpu.VMEM((clusters, clusters), jnp.int32),
            pltpu.VMEM((1, clusters), jnp.float32),
            pltpu.VMEM((8, width), jnp.int32),
            pltpu.SMEM((8, width), jnp.int32),
            pltpu.VMEM((1, width), jnp.int32),
            pltpu.VMEM((shards, 1, width), jnp.int32),
            pltpu.SMEM((shards, 1, width), jnp.int32),
            pltpu.VMEM((1, clusters), jnp.float32),
            pltpu.VMEM((shards, 1, clusters), jnp.float32),
            pltpu.VMEM((1, clusters), jnp.float32),
            pltpu.VMEM((shards, 1, clusters), jnp.float32),
            pltpu.VMEM((2 * clusters, clusters), jnp.bfloat16),
            dma((9,)),
            dma((2,)),
            dma((2,)),
            dma((2,)),
            dma((parts + 1,)),
            dma((2,)),
            dma((2,)),
            dma((shards,)),
            dma((shards,)),
        ],
        compiler_params=pltpu.CompilerParams(
            collective_id=0, has_side_effects=True, vmem_limit_bytes=56 * 2**20
        ),
        name="partition_step",
    )(
        coupling.reshape(blocks, size, clusters),
        tile_vals.reshape(blocks * slots, size, size),
        tile_cols.T,
        cluster_graph,
        cluster_mass.reshape(1, clusters),
    )
    out = pl.pallas_call(
        finish,
        out_shape=jax.ShapeDtypeStruct((blocks, size, clusters), jnp.float32),
        in_specs=[hbm, hbm],
        out_specs=hbm,
        scratch_shapes=[
            pltpu.VMEM((blocks, size, clusters), jnp.float32),
            pltpu.VMEM((1, clusters), jnp.float32),
            dma((parts + 1,)),
            dma((parts,)),
        ],
        compiler_params=pltpu.CompilerParams(vmem_limit_bytes=56 * 2**20),
        name="normalise",
    )(logits, shift)
    return out.reshape(blocks * size, clusters)


def solution(mesh):
    return jax.shard_map(
        local,
        mesh=mesh,
        in_specs=(
            P(("groups", "rows", "sub"), None),
            P(("groups", "rows", "sub"), None, None, None),
            P(("groups", "rows", "sub"), None),
            P("groups", None),
            P("groups"),
        ),
        out_specs=P(("groups", "rows", "sub"), None),
        check_vma=False,
    )
```
